512 devices in a mesh: row: 16 (over x, z_hi, core), col: 32 (over y, z_lo).
Axes of the slice: x: 4, y: 8, z: 8 (z_hi: 2, z_lo: 4; z = z_hi * 4 + z_lo), core: 2. Of those that a mesh axis runs over, the one named last changes fastest.
Arguments:
- points: float32 [8, 4, 1024], P(None, None, 'row'), may hold values from -5 to 5
- frequencies: float32 [8, 8192], replicated, may hold values from -4 to 4
- phases: float32 [8192], replicated, may hold values from -3.140625 to 3.140625
- feature_weights: bfloat16 [8192, 4096], P(None, 'col'), may hold values from -6 to 6
- observed: float32 [4, 1024, 4096], P(None, 'row', 'col'), may hold values from -6 to 6
- factor: float32 [4, 1024, 4096], P(None, 'row', 'col'), as said below
Outputs:
- solution: float32 [4, 1024, 4096], P(None, 'row', 'col')
The draws below stay inside these ranges and needn't reach their ends.
Inputs may be any that keep to these rules, and one draw needn't show every extreme that they name: `factor`: F(i, j) is zero for j > i, and F(i, i) is lower triangular with its diagonal between 0.5 and 1.5.
All inputs are finite; a program needn't handle non-finite values.
Results may differ from the reference program's by a relative error of at most 0.0017.
Values sent between devices are 32-bit elements; how exact they have to be, the bound alone decides.
No kernel may reach another device: no remote copies, remote signals or barrier semaphores. Data moves between devices by JAX's collectives and lax.ppermute only.
A program may use at most 128 MiB of HBM per device.

```python
import math
import jax
import jax.numpy as jnp
from jax import lax

BLOCK = 1024
BLOCKS = 4
FEATURES = 8192
DIM = 8
SAMPLES = 4096
COL_PIECE = 32


def draw_factor(key, part):
    key = jax.random.fold_in(key, 11)
    noise_key, pivot_key = jax.random.split(key, 2)
    shape = (BLOCKS, BLOCK, BLOCKS * BLOCK)
    noise = jnp.clip(jax.random.normal(noise_key, shape, jnp.float32), -6.0, 6.0)
    pivots = jax.random.uniform(pivot_key, shape, jnp.float32, 0.5, 1.5)
    block_row = lax.broadcasted_iota(jnp.int32, shape, 0)
    inner_row = lax.broadcasted_iota(jnp.int32, shape, 1)
    column = lax.broadcasted_iota(jnp.int32, shape, 2)
    block_col = column // BLOCK
    inner_col = column % BLOCK
    spread = 0.5 / math.sqrt(BLOCK)
    below = (block_col < block_row) | (block_col == block_row) & (inner_col < inner_row)
    on_diagonal = (block_col == block_row) & (inner_col == inner_row)
    natural = jnp.where(below, noise * spread, jnp.where(on_diagonal, pivots, 0.0))
    stored = natural.reshape(BLOCKS, BLOCK, BLOCKS, BLOCK // COL_PIECE, COL_PIECE)
    return stored.transpose(0, 1, 3, 2, 4).reshape(shape)


def shard_levels(stream_key, extent, cuts, low, largest):
    def one(position, blocks):
        steps = jax.random.uniform(jax.random.fold_in(jax.random.fold_in(stream_key, 6), position), (blocks,), jnp.float32, low / len(cuts), largest / len(cuts))
        return jnp.repeat(jnp.exp(steps), extent[position] // blocks).reshape((-1,) + (1,) * (len(extent) - position - 1))

    gain = one(*cuts[0])
    for cut in cuts[1:]:
        gain = gain * one(*cut)
    return gain


def bell_draw(stream_key, shape, width, reach, pieces=(), dtype=jnp.bfloat16):
    values = width * jax.random.normal(stream_key, shape, jnp.float32)
    if pieces:
        values = values * shard_levels(stream_key, shape, pieces, -0.22, 0.18)
    return jnp.clip(values, -reach, reach).astype(dtype)


def setup_inputs(seed: int = 0) -> dict:
    keys = jax.random.split(jax.random.key(seed), 7)
    return {
        "points": bell_draw(keys[0], (DIM, BLOCKS, BLOCK), 1.0, 5.0, ((2, 16),), jnp.float32),
        "frequencies": bell_draw(keys[1], (DIM, FEATURES), 0.7, 4.0, (), jnp.float32),
        "phases": jnp.clip(jax.random.uniform(keys[2], (FEATURES,), jnp.float32, -3.140625, 3.140625), -3.140625, 3.140625),
        "feature_weights": bell_draw(keys[3], (FEATURES, SAMPLES), 1.0, 6.0, ((1, 32),)),
        "observed": bell_draw(keys[4], (BLOCKS, BLOCK, SAMPLES), 1.0, 6.0, ((1, 16), (2, 32)), jnp.float32),
        "factor": draw_factor(jax.random.fold_in(keys[6], 71), 0),
    }


highest = lax.Precision.HIGHEST

def product(left, right):
    return jnp.dot(left, right, precision=highest, preferred_element_type=jnp.float32)

def inner_product(left, right):
    return lax.dot_general(left, right, (((0,), (0,)), ((), ())), precision=highest, preferred_element_type=jnp.float32)

def reference(points, frequencies, phases, feature_weights, observed, factor):
    natural = factor.reshape(BLOCKS, BLOCK, BLOCK // COL_PIECE, BLOCKS, COL_PIECE)
    natural = natural.transpose(0, 1, 3, 2, 4).reshape(BLOCKS, BLOCK, BLOCKS * BLOCK)
    flat_points = points.reshape(DIM, BLOCKS * BLOCK)
    angles = inner_product(flat_points, frequencies) + phases
    features = (math.sqrt(2.0 / FEATURES) * jnp.cos(angles)).astype(jnp.bfloat16)
    prior = jnp.dot(features, feature_weights, preferred_element_type=jnp.float32)
    right_side = observed - prior.reshape(BLOCKS, BLOCK, SAMPLES)
    solved = []
    for block in range(BLOCKS):
        update = right_side[block]
        for other in range(block):
            update = update - product(natural[block, :, other * BLOCK:(other + 1) * BLOCK], solved[other])
        solved.append(product(natural[block, :, block * BLOCK:(block + 1) * BLOCK], update))
    answers = [None] * BLOCKS
    for block in reversed(range(BLOCKS)):
        remain = solved[block]
        for other in range(block + 1, BLOCKS):
            remain = remain - inner_product(natural[other, :, block * BLOCK:(block + 1) * BLOCK], answers[other])
        answers[block] = inner_product(natural[block, :, block * BLOCK:(block + 1) * BLOCK], remain)
    return jnp.stack(answers)
```

```python
import math

import jax
import jax.numpy as jnp
import numpy as np
from jax import lax
from jax.experimental import pallas as pl
from jax.experimental.pallas import tpu as pltpu
from jax.sharding import Mesh
from jax.sharding import PartitionSpec as P

highest = lax.Precision.HIGHEST

SPLIT = {"x": 4, "zh": 2, "core": 2, "y": 8, "zl": 4}
ROW = ("x", "zh", "core")
COL = ("y", "zl")
Z = ("zh", "zl")

HELD = (
    ((0, 0), None, (3, 0)),
    ((1, 1), (1, 0), None),
    ((2, 2), (2, 1), (2, 0)),
    ((3, 3), (3, 2), (3, 1)),
)


def cos_coefficients():
    count = 8
    nodes = 0.125 * (1.0 - np.cos((np.arange(count) + 0.5) * np.pi / count))
    return np.polyfit(nodes * 8.0 - 1.0, np.cos(2.0 * np.pi * np.sqrt(nodes)), count - 1), nodes


def polynomial():
    fitted, _ = cos_coefficients()
    shifted = np.poly1d(fitted)(np.poly1d([8.0, -1.0]))
    return [float(c) for c in shifted.coeffs]


def feature_rows(points, frequencies, phases):
    turn = 1.0 / (2.0 * math.pi)
    rows = points.reshape(points.shape[0], -1)
    turns = lax.dot_general(
        rows, frequencies * turn, (((0,), (0,)), ((), ())), precision=highest, preferred_element_type=jnp.float32
    )
    turns = turns + phases * turn
    part = turns - jnp.round(turns)
    square = part * part
    scale = math.sqrt(2.0 / frequencies.shape[1])
    coefficients = polynomial()
    value = jnp.full_like(square, scale * coefficients[0])
    for c in coefficients[1:]:
        value = value * square + scale * c
    return value.astype(jnp.bfloat16)


def shift(size, step):
    return [(i, (i + step) % size) for i in range(size)]


def ring_gather(unit, axis, size, tasks):
    here = lax.axis_index(axis)
    held = jnp.zeros((size,) + unit.shape, unit.dtype)

    def put(held, piece, step):
        return lax.dynamic_update_slice(held, piece[None], (lax.rem(here + step + size, size),) + (0,) * unit.ndim)

    held = put(held, unit, 0)
    up = down = unit
    done = []
    for step in range(1, size // 2):
        up, down, done = lax.optimization_barrier((up, down, done))
        up = lax.ppermute(up, axis, shift(size, 1))
        down = lax.ppermute(down, axis, shift(size, -1))
        done = tasks[step - 1](done)
        up, down, done = lax.optimization_barrier((up, down, done))
        held = put(held, up, -step)
        held = put(held, down, step)
    half = unit.shape[0] // 2
    first = lax.ppermute(up[:half], axis, shift(size, 1))
    second = lax.ppermute(down[half:], axis, shift(size, -1))
    return put(held, jnp.concatenate([first, second], 0), size // 2), done


def halves(value):
    high = lax.reduce_precision(value, 8, 7)
    return high.astype(jnp.bfloat16), (value - high).astype(jnp.bfloat16)


def times(left, right, contract):
    n = left.shape[0]
    high, low = halves(left)
    dims = (((1,), (contract,)), ((), ()))
    both = lax.dot_general(jnp.concatenate([high, low], 0), right[0], dims, preferred_element_type=jnp.float32)
    rest = lax.dot_general(high, right[1], dims, preferred_element_type=jnp.float32)
    return both[:n] + both[n:] + rest


def spread_lanes(came_ref, unit_ref):
    for place in range(8):
        pieces = [came_ref[4 * place + zl] for zl in range(4)]
        for slot in range(3):
            for rows, base, start in ((slice(0, 48), slot, 0), (slice(16 * slot, 16 * slot + 16), 3, 48)):
                found = None
                for zl in range(4):
                    part = pieces[zl][rows]
                    moved = (zl - base) * 32 % 128
                    part = pltpu.roll(part, moved, 1) if moved else part
                    group = lax.broadcasted_iota(jnp.int32, part.shape, 1) // 32
                    found = part if found is None else jnp.where(group == zl, part, found)
                unit_ref[8 * slot + place, start : start + found.shape[0], :] = found


def lay_out(core_ref, own_ref, other_ref, high_ref, low_ref):
    core = core_ref[0]
    for ref, at in ((own_ref, core), (other_ref, 1 - core)):
        for place in range(ref.shape[1]):
            value = ref[0, place]
            high = value.astype(jnp.bfloat16)
            high_ref[place, at] = high
            low_ref[place, at] = (value - high.astype(jnp.float32)).astype(jnp.bfloat16)


def gather_blocks(factor, tasks):
    blocks, share, lanes = factor.shape
    k = lanes // blocks
    empty = jnp.zeros((share, k), factor.dtype)

    def piece(at):
        return empty if at is None else factor[at[0], :, at[1] * k : (at[1] + 1) * k]

    cut = share * 3 // 4
    send = []
    for slots in HELD:
        parts = [piece(at) for at in slots]
        rest = jnp.concatenate([part[cut:] for part in parts], 0)
        send.append(jnp.concatenate([part[:cut] for part in parts] + [rest], 1))
    send = jnp.broadcast_to(jnp.stack(send)[:, None], (4, 8, cut, 4 * k)).reshape(32, cut, 4 * k)
    came = lax.all_to_all(send, ("x",) + Z, 0, 0, tiled=True)
    unit = pl.pallas_call(
        spread_lanes, out_shape=jax.ShapeDtypeStruct((24, share, 4 * k), jnp.float32), name="spread_lanes"
    )(came)
    along_y, done = ring_gather(unit, "y", 8, tasks)
    other = lax.ppermute(along_y, "core", shift(2, 1))
    core = lax.axis_index("core").reshape(1).astype(jnp.int32)
    taken = pl.BlockSpec((1, 24, share, 4 * k), lambda y, core: (y, 0, 0, 0))
    given = pl.BlockSpec((24, 2, share, 4 * k), lambda y, core: (0, 0, 0, y))
    shape = jax.ShapeDtypeStruct((24, 2, share, 32 * k), jnp.bfloat16)
    both = pl.pallas_call(
        lay_out,
        grid_spec=pltpu.PrefetchScalarGridSpec(
            num_scalar_prefetch=1, grid=(8,), in_specs=[taken, taken], out_specs=[given, given]
        ),
        out_shape=[shape, shape],
        compiler_params=pltpu.CompilerParams(vmem_limit_bytes=24 * 1024 * 1024),
        name="lay_out",
    )(core, along_y, other)
    return [half.reshape(3, 16 * share, 32 * k) for half in both], done


def on_device(points, frequencies, phases, feature_weights, observed, factor):
    blocks, share, width = observed.shape
    samples = width // 4
    size = 16 * share

    def rows(which):
        def task(done):
            found = []
            for block in which:
                features = feature_rows(points[:, block], frequencies, phases)
                prior = jnp.dot(features, feature_weights, preferred_element_type=jnp.float32)
                found.append(observed[block] - prior)
            return done + found

        return task

    def send_rows(done):
        send = jnp.stack(done).reshape(blocks, share, 4, samples).transpose(0, 2, 1, 3)
        send = send.reshape(16, share * samples // 128, 128)
        came = lax.all_to_all(send, ROW, 0, 0, tiled=True)
        return [came.reshape(size, samples).T]

    (high, low), (right,) = gather_blocks(factor, [rows((0, 1)), rows((2, 3)), send_rows])
    diagonal, beside, third = [(high[slot], low[slot]) for slot in range(3)]

    here = lax.axis_index("x")

    def move(value, source, target):
        return lax.ppermute(value, "x", [(source, target)])

    first = times(right, diagonal, 1)
    near = move(first, 0, 1)
    skip = move(first, 0, 2)
    far = move(times(first, third, 1), 0, 3)
    second = times(right - times(near, beside, 1), diagonal, 1)
    near = move(second, 1, 2)
    skip_on = move(second, 1, 3)
    base = right - times(skip, third, 1)
    solved = times(base - times(near, beside, 1), diagonal, 1)
    near = move(solved, 2, 3)
    base = right - far - times(skip_on, third, 1)
    last = times(base - times(near, beside, 1), diagonal, 1)
    mine = jnp.where(here == 0, first, jnp.where(here == 1, second, jnp.where(here == 2, solved, last)))

    fourth = times(mine, diagonal, 0)
    near = move(times(fourth, beside, 0), 3, 2)
    far = move(fourth, 3, 0)
    skip = move(times(fourth, third, 0), 3, 1)
    answer = times(mine - near, diagonal, 0)
    near = move(times(answer, beside, 0), 2, 1)
    skip_on = move(times(answer, third, 0), 2, 0)
    second = times(mine - skip - near, diagonal, 0)
    near = move(times(second, beside, 0), 1, 0)
    base = mine - skip_on - times(far, third, 0)
    first = times(base - near, diagonal, 0)
    result = jnp.where(here == 0, first, jnp.where(here == 1, second, jnp.where(here == 2, answer, fourth)))

    send = result.T.reshape(16, share * samples // 128, 128)
    came = lax.all_to_all(send, ROW, 0, 0, tiled=True)
    came = came.reshape(blocks, 4, share, samples).transpose(0, 2, 1, 3)
    return came.reshape(blocks, share, width)


def solution(mesh):
    fine = Mesh(mesh.devices.reshape(tuple(SPLIT.values())), tuple(SPLIT))
    in_specs = (
        P(None, None, ROW),
        P(),
        P(),
        P(None, COL),
        P(None, ROW, COL),
        P(None, ROW, COL),
    )
    return jax.shard_map(
        on_device, mesh=fine, in_specs=in_specs, out_specs=P(None, ROW, COL), check_vma=False
    )
```

```python
import math

import jax
import jax.numpy as jnp
import numpy as np
from jax import lax
from jax.experimental import pallas as pl
from jax.experimental.pallas import tpu as pltpu
from jax.sharding import Mesh
from jax.sharding import PartitionSpec as P

highest = lax.Precision.HIGHEST

SPLIT = {"x": 4, "zh": 2, "core": 2, "y": 8, "zl": 4}
ROW = ("x", "zh", "core")
COL = ("y", "zl")
Z = ("zh", "zl")

HELD = (
    ((0, 0), None, (3, 0)),
    ((1, 1), (1, 0), None),
    ((2, 2), (2, 1), (2, 0)),
    ((3, 3), (3, 2), (3, 1)),
)


def cos_coefficients():
    count = 8
    nodes = 0.125 * (1.0 - np.cos((np.arange(count) + 0.5) * np.pi / count))
    return np.polyfit(nodes * 8.0 - 1.0, np.cos(2.0 * np.pi * np.sqrt(nodes)), count - 1), nodes


def polynomial():
    fitted, _ = cos_coefficients()
    shifted = np.poly1d(fitted)(np.poly1d([8.0, -1.0]))
    return [float(c) for c in shifted.coeffs]


def feature_rows(points, frequencies, phases):
    turn = 1.0 / (2.0 * math.pi)
    rows = points.reshape(points.shape[0], -1)
    turns = lax.dot_general(
        rows, frequencies * turn, (((0,), (0,)), ((), ())), precision=highest, preferred_element_type=jnp.float32
    )
    turns = turns + phases * turn
    part = turns - jnp.round(turns)
    square = part * part
    scale = math.sqrt(2.0 / frequencies.shape[1])
    coefficients = polynomial()
    value = jnp.full_like(square, scale * coefficients[0])
    for c in coefficients[1:]:
        value = value * square + scale * c
    return value.astype(jnp.bfloat16)


def shift(size, step):
    return [(i, (i + step) % size) for i in range(size)]


def lay_out(places_ref, own_ref, other_ref, *refs):
    core = places_ref[0]
    high_ref, low_ref = refs[-2:]
    for ref, at in ((own_ref, core), (other_ref, 1 - core)):
        for place in range(ref.shape[0]):
            value = ref[place]
            high = value.astype(jnp.bfloat16)
            high_ref[place, at] = high
            low_ref[place, at] = (value - high.astype(jnp.float32)).astype(jnp.bfloat16)


def lay(held, own, other, first, step, size):
    places, share, lanes = own.shape
    count = 12
    core, here = lax.axis_index("core"), lax.axis_index("y")
    scalars = jnp.stack([core, lax.rem(here + step + size, size)]).astype(jnp.int32)
    taken = pl.BlockSpec((count, share, lanes), lambda i, at: (i, 0, 0))
    given = pl.BlockSpec((count, 2, share, lanes), lambda i, at: (i + first // count, 0, 0, at[1]))
    shape = jax.ShapeDtypeStruct((24, 2, share, size * lanes), jnp.bfloat16)
    before = [] if held is None else list(held)
    return pl.pallas_call(
        lay_out,
        grid_spec=pltpu.PrefetchScalarGridSpec(
            num_scalar_prefetch=1,
            grid=(places // count,),
            in_specs=[taken, taken] + [pl.BlockSpec(memory_space=pl.ANY)] * len(before),
            out_specs=[given, given],
        ),
        out_shape=[shape, shape],
        input_output_aliases={3: 0, 4: 1} if before else {},
        compiler_params=pltpu.CompilerParams(vmem_limit_bytes=24 * 1024 * 1024),
        name="lay_out",
    )(scalars, own, other, *before)


def ring_gather(unit, size, ready):
    def swap(value):
        return lax.ppermute(value, "core", shift(2, 1))

    up = down = unit
    came = [(unit, 0)]
    swapped, held = [], None
    for step in range(1, size // 2 + 1):
        if step < size // 2:
            up, down = lax.ppermute(up, "y", shift(size, 1)), lax.ppermute(down, "y", shift(size, -1))
        else:
            half = unit.shape[0] // 2
            up, down = lax.ppermute(up[:half], "y", shift(size, 1)), lax.ppermute(down[half:], "y", shift(size, -1))
        others = [swap(piece) for piece, _ in came]
        for own, other, at in swapped:
            held = lay(held, own, other, 0, at, size)
        up, down, others, held, ready = lax.optimization_barrier((up, down, others, held, ready))
        swapped = [(own, other, at) for (own, at), other in zip(came, others)]
        came = [(up, -step), (down, step)]
    others = [swap(up), swap(down)]
    for own, other, at in swapped:
        held = lay(held, own, other, 0, at, size)
    held = lay(held, up, others[0], 0, size // 2, size)
    return lay(held, down, others[1], half, size // 2, size), ready


def halves(value):
    high = lax.reduce_precision(value, 8, 7)
    return high.astype(jnp.bfloat16), (value - high).astype(jnp.bfloat16)


def times(left, right, contract):
    n = left.shape[0]
    high, low = halves(left)
    dims = (((1,), (contract,)), ((), ()))
    both = lax.dot_general(jnp.concatenate([high, low], 0), right[0], dims, preferred_element_type=jnp.float32)
    rest = lax.dot_general(high, right[1], dims, preferred_element_type=jnp.float32)
    return both[:n] + both[n:] + rest


def spread_lanes(came_ref, unit_ref):
    for place in range(8):
        pieces = [came_ref[4 * place + zl] for zl in range(4)]
        for slot in range(3):
            for rows, base, start in ((slice(0, 48), slot, 0), (slice(16 * slot, 16 * slot + 16), 3, 48)):
                found = None
                for zl in range(4):
                    part = pieces[zl][rows]
                    moved = (zl - base) * 32 % 128
                    part = pltpu.roll(part, moved, 1) if moved else part
                    group = lax.broadcasted_iota(jnp.int32, part.shape, 1) // 32
                    found = part if found is None else jnp.where(group == zl, part, found)
                unit_ref[8 * slot + place, start : start + found.shape[0], :] = found


def gather_blocks(factor, ready):
    blocks, share, lanes = factor.shape
    k = lanes // blocks
    empty = jnp.zeros((share, k), factor.dtype)

    def piece(at):
        return empty if at is None else factor[at[0], :, at[1] * k : (at[1] + 1) * k]

    cut = share * 3 // 4
    send = []
    for slots in HELD:
        parts = [piece(at) for at in slots]
        rest = jnp.concatenate([part[cut:] for part in parts], 0)
        send.append(jnp.concatenate([part[:cut] for part in parts] + [rest], 1))
    send = jnp.broadcast_to(jnp.stack(send)[:, None], (4, 8, cut, 4 * k)).reshape(32, cut, 4 * k)
    came = lax.all_to_all(send, ("x",) + Z, 0, 0, tiled=True)
    unit = pl.pallas_call(
        spread_lanes, out_shape=jax.ShapeDtypeStruct((24, share, 4 * k), jnp.float32), name="spread_lanes"
    )(came)
    unit, ready = lax.optimization_barrier((unit, ready))
    held, ready = ring_gather(unit, 8, ready)
    return [half.reshape(3, 16 * share, 32 * k) for half in held], ready


def on_device(points, frequencies, phases, feature_weights, observed, factor):
    blocks, share, width = observed.shape
    samples = width // 4
    size = 16 * share

    sides = []
    for block in range(blocks):
        features = feature_rows(points[:, block], frequencies, phases)
        prior = jnp.dot(features, feature_weights, preferred_element_type=jnp.float32)
        sides.append(observed[block] - prior)
    send = jnp.stack(sides).reshape(blocks, share, 4, samples).transpose(0, 2, 1, 3)
    send = send.reshape(16, share * samples // 128, 128)
    (high, low), send = gather_blocks(factor, send)
    came = lax.all_to_all(send, ROW, 0, 0, tiled=True)
    right = came.reshape(size, samples).T
    diagonal, beside, third = [(high[slot], low[slot]) for slot in range(3)]

    here = lax.axis_index("x")

    def move(value, source, target):
        return lax.ppermute(value, "x", [(source, target)])

    first = times(right, diagonal, 1)
    near = move(first, 0, 1)
    skip = move(first, 0, 2)
    far = move(times(first, third, 1), 0, 3)
    second = times(right - times(near, beside, 1), diagonal, 1)
    near = move(second, 1, 2)
    skip_on = move(second, 1, 3)
    base = right - times(skip, third, 1)
    solved = times(base - times(near, beside, 1), diagonal, 1)
    near = move(solved, 2, 3)
    base = right - far - times(skip_on, third, 1)
    last = times(base - times(near, beside, 1), diagonal, 1)
    mine = jnp.where(here == 0, first, jnp.where(here == 1, second, jnp.where(here == 2, solved, last)))

    fourth = times(mine, diagonal, 0)
    near = move(times(fourth, beside, 0), 3, 2)
    far = move(fourth, 3, 0)
    skip = move(times(fourth, third, 0), 3, 1)
    answer = times(mine - near, diagonal, 0)
    near = move(times(answer, beside, 0), 2, 1)
    skip_on = move(times(answer, third, 0), 2, 0)
    second = times(mine - skip - near, diagonal, 0)
    near = move(times(second, beside, 0), 1, 0)
    base = mine - skip_on - times(far, third, 0)
    first = times(base - near, diagonal, 0)
    result = jnp.where(here == 0, first, jnp.where(here == 1, second, jnp.where(here == 2, answer, fourth)))

    send = result.T.reshape(16, share * samples // 128, 128)
    came = lax.all_to_all(send, ROW, 0, 0, tiled=True)
    came = came.reshape(blocks, 4, share, samples).transpose(0, 2, 1, 3)
    return came.reshape(blocks, share, width)


def solution(mesh):
    fine = Mesh(mesh.devices.reshape(tuple(SPLIT.values())), tuple(SPLIT))
    in_specs = (
        P(None, None, ROW),
        P(),
        P(),
        P(None, COL),
        P(None, ROW, COL),
        P(None, ROW, COL),
    )
    return jax.shard_map(
        on_device, mesh=fine, in_specs=in_specs, out_specs=P(None, ROW, COL), check_vma=False
    )
```

```python
import functools
import math

import jax
import jax.numpy as jnp
import numpy as np
from jax import lax
from jax.experimental import pallas as pl
from jax.experimental.pallas import tpu as pltpu
from jax.sharding import Mesh
from jax.sharding import PartitionSpec as P

highest = lax.Precision.HIGHEST

SPLIT = {"x": 4, "zh": 2, "core": 2, "y": 8, "zl": 4}
ROW = ("x", "zh", "core")
COL = ("y", "zl")
Z = ("zh", "zl")

HELD = (
    ((0, 0), None, (3, 0)),
    ((1, 1), (1, 0), None),
    ((2, 2), (2, 1), (2, 0)),
    ((3, 3), (3, 2), (3, 1)),
)


def cos_coefficients():
    count = 8
    nodes = 0.125 * (1.0 - np.cos((np.arange(count) + 0.5) * np.pi / count))
    return np.polyfit(nodes * 8.0 - 1.0, np.cos(2.0 * np.pi * np.sqrt(nodes)), count - 1), nodes


def polynomial():
    fitted, _ = cos_coefficients()
    shifted = np.poly1d(fitted)(np.poly1d([8.0, -1.0]))
    return [float(c) for c in shifted.coeffs]


def feature_rows(points, frequencies, phases):
    turn = 1.0 / (2.0 * math.pi)
    rows = points.reshape(points.shape[0], -1)
    turns = lax.dot_general(
        rows, frequencies * turn, (((0,), (0,)), ((), ())), precision=highest, preferred_element_type=jnp.float32
    )
    turns = turns + phases * turn
    part = turns - jnp.round(turns)
    square = part * part
    scale = math.sqrt(2.0 / frequencies.shape[1])
    coefficients = polynomial()
    value = jnp.full_like(square, scale * coefficients[0])
    for c in coefficients[1:]:
        value = value * square + scale * c
    return value.astype(jnp.bfloat16)


def shift(size, step):
    return [(i, (i + step) % size) for i in range(size)]


def split_piece(core_ref, *refs):
    core = core_ref[0]
    high_ref, low_ref = refs[-2:]
    start = 0
    for own_ref, other_ref in zip(refs[:-2:2], refs[1:-2:2]):
        for ref, at in ((own_ref, core), (other_ref, 1 - core)):
            for place in range(ref.shape[0]):
                value = ref[place]
                high = value.astype(jnp.bfloat16)
                high_ref[start + place, at] = high
                low_ref[start + place, at] = (value - high.astype(jnp.float32)).astype(jnp.bfloat16)
        start += own_ref.shape[0]


def split(*parts):
    share, lanes = parts[0].shape[1:]
    core = lax.axis_index("core").reshape(1).astype(jnp.int32)
    shape = jax.ShapeDtypeStruct((sum(part.shape[0] for part in parts[::2]), 2, share, lanes), jnp.bfloat16)
    whole = pl.BlockSpec(memory_space=pltpu.VMEM)
    return pl.pallas_call(
        split_piece,
        in_specs=[pl.BlockSpec(memory_space=pltpu.SMEM)] + [whole] * len(parts),
        out_specs=[whole, whole],
        out_shape=[shape, shape],
        compiler_params=pltpu.CompilerParams(vmem_limit_bytes=16 * 1024 * 1024),
        name="split_piece",
    )(core, *parts)


def ring_gather(unit, size, ready):
    def swap(value):
        return lax.ppermute(value, "core", shift(2, 1))

    up = down = unit
    came = [(unit, 0)]
    swapped, held = [], {}
    for step in range(1, size // 2 + 1):
        if step < size // 2:
            up, down = lax.ppermute(up, "y", shift(size, 1)), lax.ppermute(down, "y", shift(size, -1))
        else:
            half = unit.shape[0] // 2
            up, down = lax.ppermute(up[:half], "y", shift(size, 1)), lax.ppermute(down[half:], "y", shift(size, -1))
        others = [swap(piece) for piece, _ in came]
        fresh = [split(own, other) for own, other, _ in swapped]
        up, down, others, fresh, ready = lax.optimization_barrier((up, down, others, fresh, ready))
        held.update((at, both) for (_, _, at), both in zip(swapped, fresh))
        swapped = [(own, other, at) for (own, at), other in zip(came, others)]
        came = [(up, -step), (down, step)]
    others = [swap(up), swap(down)]
    held.update((at, split(own, other)) for own, other, at in swapped)
    held[size // 2] = split(up, others[0], down, others[1])
    return held, ready


def multiply(steps, forward, first, last, here_ref, left_ref, *refs):
    count = len(steps)
    taken = list(refs)
    take_ref = taken.pop(0) if first else None
    base_ref = taken.pop(0) if last else None
    highs, lows = taken[:count], taken[count : 2 * count]
    out_ref, value_ref, parts_ref = taken[2 * count :]
    n = left_ref.shape[0]
    turn = pl.program_id(0)

    @pl.when(turn == 0)
    def _():
        value_ref[...] = left_ref[...] - take_ref[...] if first else left_ref[...]

    value = value_ref[...]
    high = value.astype(jnp.bfloat16)
    parts_ref[:n] = high
    parts_ref[n:] = (value - high.astype(jnp.float32)).astype(jnp.bfloat16)
    columns = [pl.ds(pl.multiple_of(lax.rem(here_ref[0] + at + count, count) * 128, 128), 128) for at in steps]

    def add(left, high, low, contract):
        dims = (((1,), (contract,)), ((), ()))
        both = lax.dot_general(left, high, dims, preferred_element_type=jnp.float32)
        return both[:n] + both[n:] + lax.dot_general(left[:n], low, dims, preferred_element_type=jnp.float32)

    if forward:
        for place in range(0, 8, 2):
            total = None
            for pair in range(0, count, 2):
                left = jnp.concatenate([parts_ref[:, columns[i]] for i in (pair, pair + 1)], 1)
                high, low = (
                    jnp.concatenate([ref[i][place : place + 2].reshape(256, 128) for i in (pair, pair + 1)], 1)
                    for ref in (highs, lows)
                )
                part = add(left, high, low, 1)
                total = part if total is None else total + part
            value_ref[:, place * 128 : place * 128 + 256] = total
    else:
        left = parts_ref[...]
        for pair in range(0, count, 2):
            high, low = (
                jnp.concatenate([ref[i][...].reshape(1024, 128) for i in (pair, pair + 1)], 1) for ref in (highs, lows)
            )
            part = add(left, high, low, 0)
            value_ref[:, columns[pair]] = part[:, :128]
            value_ref[:, columns[pair + 1]] = part[:, 128:]

    if last:

        @pl.when(turn == 0)
        def _():
            value_ref[...] = base_ref[...] - value_ref[...]

    out_ref[0] = value_ref[...]


def times(held, slots, forward, left, take=None, base=None):
    steps = sorted(held)
    n, size = left.shape
    extra = [value for value in (take, base) if value is not None]
    highs, lows = [held[at][0] for at in steps], [held[at][1] for at in steps]
    small = pl.BlockSpec((n, size), lambda i, here: (0, 0))
    stride = slots[-1] - slots[0]
    block = pl.BlockSpec((8,) + highs[0].shape[1:], lambda i, here: (slots[0] + i * stride, 0, 0, 0))
    here = lax.axis_index("y").reshape(1).astype(jnp.int32)
    return pl.pallas_call(
        functools.partial(multiply, steps, forward, take is not None, base is not None),
        grid_spec=pltpu.PrefetchScalarGridSpec(
            num_scalar_prefetch=1,
            grid=(len(slots),),
            in_specs=[small] * (1 + len(extra)) + [block] * (2 * len(steps)),
            out_specs=pl.BlockSpec((1, n, size), lambda i, here: (i, 0, 0)),
            scratch_shapes=[pltpu.VMEM((n, size), jnp.float32), pltpu.VMEM((2 * n, size), jnp.bfloat16)],
        ),
        out_shape=jax.ShapeDtypeStruct((len(slots), n, size), jnp.float32),
        compiler_params=pltpu.CompilerParams(vmem_limit_bytes=24 * 1024 * 1024),
        name="times",
    )(here, left, *extra, *highs, *lows)


def spread_lanes(came_ref, unit_ref):
    for place in range(8):
        pieces = [came_ref[4 * place + zl] for zl in range(4)]
        for slot in range(3):
            for rows, base, start in ((slice(0, 48), slot, 0), (slice(16 * slot, 16 * slot + 16), 3, 48)):
                found = None
                for zl in range(4):
                    part = pieces[zl][rows]
                    moved = (zl - base) * 32 % 128
                    part = pltpu.roll(part, moved, 1) if moved else part
                    group = lax.broadcasted_iota(jnp.int32, part.shape, 1) // 32
                    found = part if found is None else jnp.where(group == zl, part, found)
                unit_ref[8 * slot + place, start : start + found.shape[0], :] = found


def gather_blocks(factor, ready):
    blocks, share, lanes = factor.shape
    k = lanes // blocks
    empty = jnp.zeros((share, k), factor.dtype)

    def piece(at):
        return empty if at is None else factor[at[0], :, at[1] * k : (at[1] + 1) * k]

    cut = share * 3 // 4
    send = []
    for slots in HELD:
        parts = [piece(at) for at in slots]
        rest = jnp.concatenate([part[cut:] for part in parts], 0)
        send.append(jnp.concatenate([part[:cut] for part in parts] + [rest], 1))
    send = jnp.broadcast_to(jnp.stack(send)[:, None], (4, 8, cut, 4 * k)).reshape(32, cut, 4 * k)
    came = lax.all_to_all(send, ("x",) + Z, 0, 0, tiled=True)
    unit = pl.pallas_call(
        spread_lanes, out_shape=jax.ShapeDtypeStruct((24, share, 4 * k), jnp.float32), name="spread_lanes"
    )(came)
    unit, ready = lax.optimization_barrier((unit, ready))
    held, ready = ring_gather(unit, 8, ready)
    return held, ready


def on_device(points, frequencies, phases, feature_weights, observed, factor):
    blocks, share, width = observed.shape
    samples = width // 4
    size = 16 * share

    sides = []
    for block in range(blocks):
        features = feature_rows(points[:, block], frequencies, phases)
        prior = jnp.dot(features, feature_weights, preferred_element_type=jnp.float32)
        sides.append(observed[block] - prior)
    send = jnp.stack(sides).reshape(blocks, share, 4, samples).transpose(0, 2, 1, 3)
    send = send.reshape(16, share * samples // 128, 128)
    held, send = gather_blocks(factor, send)
    came = lax.all_to_all(send, ROW, 0, 0, tiled=True)
    right = came.reshape(size, samples).T
    here = lax.axis_index("x")

    def move(value, source, target):
        return lax.ppermute(value, "x", [(source, target)])

    def forth(near, base):
        return times(held, (1, 0), True, near, base=base)[1]

    def back(near, base):
        return times(held, (0, 1), False, base, take=near)

    first = times(held, (0,), True, right)[0]
    near = move(first, 0, 1)
    skip = move(first, 0, 2)
    far = move(times(held, (2,), True, first)[0], 0, 3)
    second = forth(near, right)
    near = move(second, 1, 2)
    skip_on = move(second, 1, 3)
    solved = forth(near, times(held, (2,), True, skip, base=right)[0])
    near = move(solved, 2, 3)
    last = forth(near, times(held, (2,), True, skip_on, base=right - far)[0])
    mine = jnp.where(here == 0, first, jnp.where(here == 1, second, jnp.where(here == 2, solved, last)))

    fourth, near = times(held, (0, 1), False, mine)
    near = move(near, 3, 2)
    far = move(fourth, 3, 0)
    skip = move(times(held, (2,), False, fourth)[0], 3, 1)
    answer, near = back(near, mine)
    near = move(near, 2, 1)
    skip_on = move(times(held, (2,), False, answer)[0], 2, 0)
    second, near = back(near, mine - skip)
    near = move(near, 1, 0)
    base = times(held, (2,), False, far, base=mine - skip_on)[0]
    first = times(held, (0,), False, base, take=near)[0]
    result = jnp.where(here == 0, first, jnp.where(here == 1, second, jnp.where(here == 2, answer, fourth)))

    send = result.T.reshape(16, share * samples // 128, 128)
    came = lax.all_to_all(send, ROW, 0, 0, tiled=True)
    came = came.reshape(blocks, 4, share, samples).transpose(0, 2, 1, 3)
    return came.reshape(blocks, share, width)


def solution(mesh):
    fine = Mesh(mesh.devices.reshape(tuple(SPLIT.values())), tuple(SPLIT))
    in_specs = (
        P(None, None, ROW),
        P(),
        P(),
        P(None, COL),
        P(None, ROW, COL),
        P(None, ROW, COL),
    )
    return jax.shard_map(
        on_device, mesh=fine, in_specs=in_specs, out_specs=P(None, ROW, COL), check_vma=False
    )
```

```python
import functools
import math

import jax
import jax.numpy as jnp
import numpy as np
from jax import lax
from jax.experimental import pallas as pl
from jax.experimental.pallas import tpu as pltpu
from jax.sharding import Mesh
from jax.sharding import PartitionSpec as P

highest = lax.Precision.HIGHEST

SPLIT = {"x": 4, "zh": 2, "core": 2, "y": 8, "zl": 4}
ROW = ("x", "zh", "core")
COL = ("y", "zl")
Z = ("zh", "zl")

HELD = (
    ((0, 0), None, (3, 0)),
    ((1, 1), (1, 0), None),
    ((2, 2), (2, 1), (2, 0)),
    ((3, 3), (3, 2), (3, 1)),
)


def cos_coefficients():
    count = 8
    nodes = 0.125 * (1.0 - np.cos((np.arange(count) + 0.5) * np.pi / count))
    return np.polyfit(nodes * 8.0 - 1.0, np.cos(2.0 * np.pi * np.sqrt(nodes)), count - 1), nodes


def polynomial():
    fitted, _ = cos_coefficients()
    shifted = np.poly1d(fitted)(np.poly1d([8.0, -1.0]))
    return [float(c) for c in shifted.coeffs]


def feature_rows(points, frequencies, phases):
    turn = 1.0 / (2.0 * math.pi)
    rows = points.reshape(points.shape[0], -1)
    turns = lax.dot_general(
        rows, frequencies * turn, (((0,), (0,)), ((), ())), precision=highest, preferred_element_type=jnp.float32
    )
    turns = turns + phases * turn
    part = turns - jnp.round(turns)
    square = part * part
    scale = math.sqrt(2.0 / frequencies.shape[1])
    coefficients = polynomial()
    value = jnp.full_like(square, scale * coefficients[0])
    for c in coefficients[1:]:
        value = value * square + scale * c
    return value.astype(jnp.bfloat16)


def shift(size, step):
    return [(i, (i + step) % size) for i in range(size)]


def lay_out(steps, places_ref, *refs):
    core, here = places_ref[0], places_ref[1]
    high_ref, low_ref = refs[-2:]
    size = len(steps)
    late = pl.program_id(0) >= 3
    for i, step in enumerate(steps):
        column = pl.ds(pl.multiple_of(lax.rem(here + step + size, size) * 128, 128), 128)
        for j, at in ((0, core), (1, 1 - core)):
            for place in range(high_ref.shape[0]):
                value = refs[2 * i + j][place]
                if 2 * step == size:
                    value = jnp.where(late, refs[2 * i + 2 + j][place], value)
                high = value.astype(jnp.bfloat16)
                high_ref[place, at, :, column] = high
                low_ref[place, at, :, column] = (value - high.astype(jnp.float32)).astype(jnp.bfloat16)


def lay(pieces, size):
    share, lanes = pieces[0][1].shape[1:]
    steps = [step for step, _, _ in pieces[:-1]]
    core, here = lax.axis_index("core"), lax.axis_index("y")
    scalars = jnp.stack([core, here]).astype(jnp.int32)
    count = 4
    full = pl.BlockSpec((count, share, lanes), lambda i, at: (i, 0, 0))
    early = pl.BlockSpec((count, share, lanes), lambda i, at: (jnp.minimum(i, 2), 0, 0))
    late = pl.BlockSpec((count, share, lanes), lambda i, at: (jnp.maximum(i - 3, 0), 0, 0))
    given = pl.BlockSpec((count, 2, share, size * lanes), lambda i, at: (i, 0, 0, 0))
    shape = jax.ShapeDtypeStruct((24, 2, share, size * lanes), jnp.bfloat16)
    return pl.pallas_call(
        functools.partial(lay_out, steps),
        grid_spec=pltpu.PrefetchScalarGridSpec(
            num_scalar_prefetch=1,
            grid=(24 // count,),
            in_specs=[full] * (2 * len(pieces) - 4) + [early] * 2 + [late] * 2,
            out_specs=[given, given],
        ),
        out_shape=[shape, shape],
        compiler_params=pltpu.CompilerParams(vmem_limit_bytes=63 * 1024 * 1024),
        name="lay_out",
    )(scalars, *[value for _, own, other in pieces for value in (own, other)])


def ring_gather(unit, size, right):
    def swap(value):
        return lax.ppermute(value, "core", shift(2, 1))

    up = down = unit
    came = [(0, unit)]
    pieces = []
    for step in range(1, size // 2 + 1):
        if step < size // 2:
            up, down = lax.ppermute(up, "y", shift(size, 1)), lax.ppermute(down, "y", shift(size, -1))
        else:
            half = unit.shape[0] // 2
            up, down = lax.ppermute(up[:half], "y", shift(size, 1)), lax.ppermute(down[half:], "y", shift(size, -1))
        others = [swap(piece) for _, piece in came]
        up, down, others, right = lax.optimization_barrier((up, down, others, right))
        pieces += [(at, own, other) for (at, own), other in zip(came, others)]
        came = [(-step, up), (step, down)]
    pieces += [(size // 2, up, swap(up)), (size // 2, down, swap(down))]
    return pieces, right


def halves(value):
    high = lax.reduce_precision(value, 8, 7)
    return high.astype(jnp.bfloat16), (value - high).astype(jnp.bfloat16)


def times(left, right, contract):
    n = left.shape[0]
    high, low = halves(left)
    dims = (((1,), (contract,)), ((), ()))
    both = lax.dot_general(jnp.concatenate([high, low], 0), right[0], dims, preferred_element_type=jnp.float32)
    rest = lax.dot_general(high, right[1], dims, preferred_element_type=jnp.float32)
    return both[:n] + both[n:] + rest


def spread_lanes(came_ref, unit_ref):
    for place in range(8):
        pieces = [came_ref[4 * place + zl] for zl in range(4)]
        for slot in range(3):
            for rows, base, start in ((slice(0, 48), slot, 0), (slice(16 * slot, 16 * slot + 16), 3, 48)):
                found = None
                for zl in range(4):
                    part = pieces[zl][rows]
                    moved = (zl - base) * 32 % 128
                    part = pltpu.roll(part, moved, 1) if moved else part
                    group = lax.broadcasted_iota(jnp.int32, part.shape, 1) // 32
                    found = part if found is None else jnp.where(group == zl, part, found)
                unit_ref[8 * slot + place, start : start + found.shape[0], :] = found


def gather_blocks(factor, sides, send_sides):
    blocks, share, lanes = factor.shape
    k = lanes // blocks
    empty = jnp.zeros((share, k), factor.dtype)

    def piece(at):
        return empty if at is None else factor[at[0], :, at[1] * k : (at[1] + 1) * k]

    cut = share * 3 // 4
    send = []
    for slots in HELD:
        parts = [piece(at) for at in slots]
        rest = jnp.concatenate([part[cut:] for part in parts], 0)
        send.append(jnp.concatenate([part[:cut] for part in parts] + [rest], 1))
    send = jnp.broadcast_to(jnp.stack(send)[:, None], (4, 8, cut, 4 * k)).reshape(32, cut, 4 * k)
    came = lax.all_to_all(send, ("x",) + Z, 0, 0, tiled=True)
    came, sides = lax.optimization_barrier((came, sides))
    right = send_sides(sides)
    unit = pl.pallas_call(
        spread_lanes,
        out_shape=jax.ShapeDtypeStruct((24, share, 4 * k), jnp.float32),
        compiler_params=pltpu.CompilerParams(vmem_limit_bytes=16 * 1024 * 1024),
        name="spread_lanes",
    )(came)
    pieces, right = ring_gather(unit, 8, right)
    return [half.reshape(3, 16 * share, 32 * k) for half in lay(pieces, 8)], right


def on_device(points, frequencies, phases, feature_weights, observed, factor):
    blocks, share, width = observed.shape
    samples = width // 4
    size = 16 * share

    sides = []
    for block in range(blocks):
        features = feature_rows(points[:, block], frequencies, phases)
        prior = jnp.dot(features, feature_weights, preferred_element_type=jnp.float32)
        sides.append(observed[block] - prior)
    send = jnp.stack(sides).reshape(blocks, share, 4, samples).transpose(0, 2, 1, 3)
    send = send.reshape(16, share * samples // 128, 128)

    def send_sides(send):
        came = lax.all_to_all(send, ROW, 0, 0, tiled=True)
        return came.reshape(size, samples).T

    (high, low), right = gather_blocks(factor, send, send_sides)
    diagonal, beside, third = [(high[slot], low[slot]) for slot in range(3)]

    here = lax.axis_index("x")

    def move(value, source, target):
        return lax.ppermute(value, "x", [(source, target)])

    first = times(right, diagonal, 1)
    near = move(first, 0, 1)
    skip = move(first, 0, 2)
    far = move(times(first, third, 1), 0, 3)
    second = times(right - times(near, beside, 1), diagonal, 1)
    near = move(second, 1, 2)
    skip_on = move(second, 1, 3)
    base = right - times(skip, third, 1)
    solved = times(base - times(near, beside, 1), diagonal, 1)
    near = move(solved, 2, 3)
    base = right - far - times(skip_on, third, 1)
    last = times(base - times(near, beside, 1), diagonal, 1)
    mine = jnp.where(here == 0, first, jnp.where(here == 1, second, jnp.where(here == 2, solved, last)))

    fourth = times(mine, diagonal, 0)
    near = move(times(fourth, beside, 0), 3, 2)
    far = move(fourth, 3, 0)
    skip = move(times(fourth, third, 0), 3, 1)
    answer = times(mine - near, diagonal, 0)
    near = move(times(answer, beside, 0), 2, 1)
    skip_on = move(times(answer, third, 0), 2, 0)
    second = times(mine - skip - near, diagonal, 0)
    near = move(times(second, beside, 0), 1, 0)
    base = mine - skip_on - times(far, third, 0)
    first = times(base - near, diagonal, 0)
    result = jnp.where(here == 0, first, jnp.where(here == 1, second, jnp.where(here == 2, answer, fourth)))

    send = result.T.reshape(16, share * samples // 128, 128)
    came = lax.all_to_all(send, ROW, 0, 0, tiled=True)
    came = came.reshape(blocks, 4, share, samples).transpose(0, 2, 1, 3)
    return came.reshape(blocks, share, width)


def solution(mesh):
    fine = Mesh(mesh.devices.reshape(tuple(SPLIT.values())), tuple(SPLIT))
    in_specs = (
        P(None, None, ROW),
        P(),
        P(),
        P(None, COL),
        P(None, ROW, COL),
        P(None, ROW, COL),
    )
    return jax.shard_map(
        on_device, mesh=fine, in_specs=in_specs, out_specs=P(None, ROW, COL), check_vma=False
    )
```

```python
import math

import jax
import jax.numpy as jnp
import numpy as np
from jax import lax
from jax.experimental import pallas as pl
from jax.experimental.pallas import tpu as pltpu
from jax.sharding import Mesh
from jax.sharding import PartitionSpec as P

highest = lax.Precision.HIGHEST

SPLIT = {"x": 4, "zh": 2, "core": 2, "y": 8, "zl": 4}
ROW = ("x", "zh", "core")
COL = ("y", "zl")
Z = ("zh", "zl")

HELD = (
    ((0, 0), None, (3, 0)),
    ((1, 1), (1, 0), None),
    ((2, 2), (2, 1), (2, 0)),
    ((3, 3), (3, 2), (3, 1)),
)


def cos_coefficients():
    count = 8
    nodes = 0.125 * (1.0 - np.cos((np.arange(count) + 0.5) * np.pi / count))
    return np.polyfit(nodes * 8.0 - 1.0, np.cos(2.0 * np.pi * np.sqrt(nodes)), count - 1), nodes


def polynomial():
    fitted, _ = cos_coefficients()
    shifted = np.poly1d(fitted)(np.poly1d([8.0, -1.0]))
    return [float(c) for c in shifted.coeffs]


def feature_rows(points, frequencies, phases):
    turn = 1.0 / (2.0 * math.pi)
    rows = points.reshape(points.shape[0], -1)
    turns = lax.dot_general(
        rows, frequencies * turn, (((0,), (0,)), ((), ())), precision=highest, preferred_element_type=jnp.float32
    )
    turns = turns + phases * turn
    part = turns - jnp.round(turns)
    square = part * part
    scale = math.sqrt(2.0 / frequencies.shape[1])
    coefficients = polynomial()
    value = jnp.full_like(square, scale * coefficients[0])
    for c in coefficients[1:]:
        value = value * square + scale * c
    return value.astype(jnp.bfloat16)


def shift(size, step):
    return [(i, (i + step) % size) for i in range(size)]


def ring_gather(unit, axis, size, parts, beside):
    here = lax.axis_index(axis)
    rows = unit.shape[0] // parts
    held = [jnp.zeros((size, rows) + unit.shape[1:], unit.dtype) for _ in range(parts)]

    def put(held, piece, step):
        at = (lax.rem(here + step + size, size),) + (0,) * unit.ndim
        return [
            lax.dynamic_update_slice(part, piece[None, i * rows : (i + 1) * rows], at) for i, part in enumerate(held)
        ]

    held = put(held, unit, 0)
    up = down = unit
    result = None
    for step in range(1, size // 2):
        up = lax.ppermute(up, axis, shift(size, 1))
        down = lax.ppermute(down, axis, shift(size, -1))
        if step == 1:
            result = beside()
        up, down, result = lax.optimization_barrier((up, down, result))
        held = put(held, up, -step)
        held = put(held, down, step)
    half = unit.shape[0] // 2
    first = lax.ppermute(up[:half], axis, shift(size, 1))
    second = lax.ppermute(down[half:], axis, shift(size, -1))
    return put(held, jnp.concatenate([first, second], 0), size // 2), result


def halves(value):
    high = lax.reduce_precision(value, 8, 7)
    return high.astype(jnp.bfloat16), (value - high).astype(jnp.bfloat16)


def times(left, right, contract):
    n = left.shape[0]
    high, low = halves(left)
    dims = (((1,), (contract,)), ((), ()))
    both = lax.dot_general(jnp.concatenate([high, low], 0), right[0], dims, preferred_element_type=jnp.float32)
    rest = lax.dot_general(high, right[1], dims, preferred_element_type=jnp.float32)
    return both[:n] + both[n:] + rest


def spread_lanes(came_ref, unit_ref):
    for place in range(8):
        pieces = [came_ref[4 * place + zl] for zl in range(4)]
        for slot in range(3):
            for rows, base, start in ((slice(0, 48), slot, 0), (slice(16 * slot, 16 * slot + 16), 3, 48)):
                found = None
                for zl in range(4):
                    part = pieces[zl][rows]
                    moved = (zl - base) * 32 % 128
                    part = pltpu.roll(part, moved, 1) if moved else part
                    group = lax.broadcasted_iota(jnp.int32, part.shape, 1) // 32
                    found = part if found is None else jnp.where(group == zl, part, found)
                unit_ref[8 * slot + place, start : start + found.shape[0], :] = found


def lay_out(core_ref, own_ref, other_ref, high_ref, low_ref):
    core = core_ref[0]
    for ref, at in ((own_ref, core), (other_ref, 1 - core)):
        for place in range(ref.shape[1]):
            value = ref[0, place]
            high = value.astype(jnp.bfloat16)
            high_ref[place, at] = high
            low_ref[place, at] = (value - high.astype(jnp.float32)).astype(jnp.bfloat16)


def gather_blocks(factor, sides, send_sides):
    blocks, share, lanes = factor.shape
    k = lanes // blocks
    empty = jnp.zeros((share, k), factor.dtype)

    def piece(at):
        return empty if at is None else factor[at[0], :, at[1] * k : (at[1] + 1) * k]

    cut = share * 3 // 4
    send = []
    for slots in HELD:
        parts = [piece(at) for at in slots]
        rest = jnp.concatenate([part[cut:] for part in parts], 0)
        send.append(jnp.concatenate([part[:cut] for part in parts] + [rest], 1))
    send = jnp.broadcast_to(jnp.stack(send)[:, None], (4, 8, cut, 4 * k)).reshape(32, cut, 4 * k)
    came = lax.all_to_all(send, ("x",) + Z, 0, 0, tiled=True)
    unit = pl.pallas_call(
        spread_lanes,
        out_shape=jax.ShapeDtypeStruct((24, share, 4 * k), jnp.float32),
        compiler_params=pltpu.CompilerParams(vmem_limit_bytes=16 * 1024 * 1024),
        name="spread_lanes",
    )(came)
    unit, sides = lax.optimization_barrier((unit, sides))
    held, right = ring_gather(unit, "y", 8, 3, lambda: send_sides(sides))
    core = lax.axis_index("core").reshape(1).astype(jnp.int32)
    taken = pl.BlockSpec((1, 8, share, 4 * k), lambda y, core: (y, 0, 0, 0))
    given = pl.BlockSpec((8, 2, share, 4 * k), lambda y, core: (0, 0, 0, y))
    shape = jax.ShapeDtypeStruct((8, 2, share, 32 * k), jnp.bfloat16)
    others = [lax.ppermute(part, "core", shift(2, 1)) for part in held]
    found = []
    for own, other in zip(held, others):
        both = pl.pallas_call(
            lay_out,
            grid_spec=pltpu.PrefetchScalarGridSpec(
                num_scalar_prefetch=1, grid=(8,), in_specs=[taken, taken], out_specs=[given, given]
            ),
            out_shape=[shape, shape],
            compiler_params=pltpu.CompilerParams(vmem_limit_bytes=16 * 1024 * 1024),
            name="lay_out",
        )(core, own, other)
        found.append(tuple(half.reshape(16 * share, 32 * k) for half in both))
    return found, right


def on_device(points, frequencies, phases, feature_weights, observed, factor):
    blocks, share, width = observed.shape
    samples = width // 4
    size = 16 * share

    sides = []
    for block in range(blocks):
        features = feature_rows(points[:, block], frequencies, phases)
        prior = jnp.dot(features, feature_weights, preferred_element_type=jnp.float32)
        sides.append(observed[block] - prior)
    send = jnp.stack(sides).reshape(blocks, share, 4, samples).transpose(0, 2, 1, 3)
    send = send.reshape(16, share * samples // 128, 128)

    def send_sides(send):
        came = lax.all_to_all(send, ROW, 0, 0, tiled=True)
        return came.reshape(size, samples).T

    (diagonal, beside, third), right = gather_blocks(factor, send, send_sides)

    here = lax.axis_index("x")

    def move(value, source, target):
        return lax.ppermute(value, "x", [(source, target)])

    first = times(right, diagonal, 1)
    near = move(first, 0, 1)
    skip = move(first, 0, 2)
    far = move(times(first, third, 1), 0, 3)
    second = times(right - times(near, beside, 1), diagonal, 1)
    near = move(second, 1, 2)
    skip_on = move(second, 1, 3)
    base = right - times(skip, third, 1)
    solved = times(base - times(near, beside, 1), diagonal, 1)
    near = move(solved, 2, 3)
    base = right - far - times(skip_on, third, 1)
    last = times(base - times(near, beside, 1), diagonal, 1)
    mine = jnp.where(here == 0, first, jnp.where(here == 1, second, jnp.where(here == 2, solved, last)))

    fourth = times(mine, diagonal, 0)
    near = move(times(fourth, beside, 0), 3, 2)
    far = move(fourth, 3, 0)
    skip = move(times(fourth, third, 0), 3, 1)
    answer = times(mine - near, diagonal, 0)
    near = move(times(answer, beside, 0), 2, 1)
    skip_on = move(times(answer, third, 0), 2, 0)
    second = times(mine - skip - near, diagonal, 0)
    near = move(times(second, beside, 0), 1, 0)
    base = mine - skip_on - times(far, third, 0)
    first = times(base - near, diagonal, 0)
    result = jnp.where(here == 0, first, jnp.where(here == 1, second, jnp.where(here == 2, answer, fourth)))

    send = result.T.reshape(16, share * samples // 128, 128)
    came = lax.all_to_all(send, ROW, 0, 0, tiled=True)
    came = came.reshape(blocks, 4, share, samples).transpose(0, 2, 1, 3)
    return came.reshape(blocks, share, width)


def solution(mesh):
    fine = Mesh(mesh.devices.reshape(tuple(SPLIT.values())), tuple(SPLIT))
    in_specs = (
        P(None, None, ROW),
        P(),
        P(),
        P(None, COL),
        P(None, ROW, COL),
        P(None, ROW, COL),
    )
    return jax.shard_map(
        on_device, mesh=fine, in_specs=in_specs, out_specs=P(None, ROW, COL), check_vma=False
    )
```

```python
import math

import jax
import jax.numpy as jnp
import numpy as np
from jax import lax
from jax.experimental import pallas as pl
from jax.experimental.pallas import tpu as pltpu
from jax.sharding import Mesh
from jax.sharding import PartitionSpec as P

highest = lax.Precision.HIGHEST

SPLIT = {"x": 4, "zh": 2, "core": 2, "y": 8, "zl": 4}
ROW = ("x", "zh", "core")
COL = ("y", "zl")
Z = ("zh", "zl")

HELD = (
    ((0, 0), None, (3, 0)),
    ((1, 1), (1, 0), None),
    ((2, 2), (2, 1), (2, 0)),
    ((3, 3), (3, 2), (3, 1)),
)


def cos_coefficients():
    count = 8
    nodes = 0.125 * (1.0 - np.cos((np.arange(count) + 0.5) * np.pi / count))
    return np.polyfit(nodes * 8.0 - 1.0, np.cos(2.0 * np.pi * np.sqrt(nodes)), count - 1), nodes


def polynomial():
    fitted, _ = cos_coefficients()
    shifted = np.poly1d(fitted)(np.poly1d([8.0, -1.0]))
    return [float(c) for c in shifted.coeffs]


def feature_rows(points, frequencies, phases):
    turn = 1.0 / (2.0 * math.pi)
    rows = points.reshape(points.shape[0], -1)
    turns = lax.dot_general(
        rows, frequencies * turn, (((0,), (0,)), ((), ())), precision=highest, preferred_element_type=jnp.float32
    )
    turns = turns + phases * turn
    part = turns - jnp.round(turns)
    square = part * part
    scale = math.sqrt(2.0 / frequencies.shape[1])
    coefficients = polynomial()
    value = jnp.full_like(square, scale * coefficients[0])
    for c in coefficients[1:]:
        value = value * square + scale * c
    return value.astype(jnp.bfloat16)


def shift(size, step):
    return [(i, (i + step) % size) for i in range(size)]


def ring_gather(unit, axis, size, parts, beside):
    here = lax.axis_index(axis)
    rows = unit.shape[0] // parts
    held = [jnp.zeros((size, rows) + unit.shape[1:], unit.dtype) for _ in range(parts)]

    def put(held, piece, step):
        at = (lax.rem(here + step + size, size),) + (0,) * unit.ndim
        return [
            lax.dynamic_update_slice(part, piece[None, i * rows : (i + 1) * rows], at) for i, part in enumerate(held)
        ]

    held = put(held, unit, 0)
    up = down = unit
    result = None
    for step in range(1, size // 2):
        up = lax.ppermute(up, axis, shift(size, 1))
        down = lax.ppermute(down, axis, shift(size, -1))
        if step == 1:
            result = beside()
            down, result = lax.optimization_barrier((down, result))
        held = put(held, up, -step)
        held = put(held, down, step)
    half = unit.shape[0] // 2
    first = lax.ppermute(up[:half], axis, shift(size, 1))
    second = lax.ppermute(down[half:], axis, shift(size, -1))
    return put(held, jnp.concatenate([first, second], 0), size // 2), result


def halves(value):
    high = lax.reduce_precision(value, 8, 7)
    return high.astype(jnp.bfloat16), (value - high).astype(jnp.bfloat16)


def times(left, right, contract):
    n = left.shape[0]
    high, low = halves(left)
    dims = (((1,), (contract,)), ((), ()))
    both = lax.dot_general(jnp.concatenate([high, low], 0), right[0], dims, preferred_element_type=jnp.float32)
    rest = lax.dot_general(high, right[1], dims, preferred_element_type=jnp.float32)
    return both[:n] + both[n:] + rest


def spread_lanes(came_ref, unit_ref):
    for place in range(8):
        pieces = [came_ref[4 * place + zl] for zl in range(4)]
        for slot in range(3):
            for rows, base, start in ((slice(0, 48), slot, 0), (slice(16 * slot, 16 * slot + 16), 3, 48)):
                found = None
                for zl in range(4):
                    part = pieces[zl][rows]
                    moved = (zl - base) * 32 % 128
                    part = pltpu.roll(part, moved, 1) if moved else part
                    group = lax.broadcasted_iota(jnp.int32, part.shape, 1) // 32
                    found = part if found is None else jnp.where(group == zl, part, found)
                unit_ref[8 * slot + place, start : start + found.shape[0], :] = found


def lay_out(core_ref, own_ref, other_ref, high_ref, low_ref):
    core = core_ref[0]

    def one(place, carry):
        for ref, at in ((own_ref, core), (other_ref, 1 - core)):
            for y in range(ref.shape[0]):
                value = ref[y, place]
                high = value.astype(jnp.bfloat16)
                high_ref[place, at, :, 128 * y : 128 * y + 128] = high
                low_ref[place, at, :, 128 * y : 128 * y + 128] = (value - high.astype(jnp.float32)).astype(jnp.bfloat16)
        return carry

    lax.fori_loop(0, own_ref.shape[1], one, 0)


def gather_blocks(factor, sides, send_sides):
    blocks, share, lanes = factor.shape
    k = lanes // blocks
    empty = jnp.zeros((share, k), factor.dtype)

    def piece(at):
        return empty if at is None else factor[at[0], :, at[1] * k : (at[1] + 1) * k]

    cut = share * 3 // 4
    send = []
    for slots in HELD:
        parts = [piece(at) for at in slots]
        rest = jnp.concatenate([part[cut:] for part in parts], 0)
        send.append(jnp.concatenate([part[:cut] for part in parts] + [rest], 1))
    send = jnp.broadcast_to(jnp.stack(send)[:, None], (4, 8, cut, 4 * k)).reshape(32, cut, 4 * k)
    came = lax.all_to_all(send, ("x",) + Z, 0, 0, tiled=True)
    unit = pl.pallas_call(
        spread_lanes,
        out_shape=jax.ShapeDtypeStruct((24, share, 4 * k), jnp.float32),
        compiler_params=pltpu.CompilerParams(vmem_limit_bytes=16 * 1024 * 1024),
        name="spread_lanes",
    )(came)
    unit, sides = lax.optimization_barrier((unit, sides))
    held, right = ring_gather(unit, "y", 8, 3, lambda: send_sides(sides))
    core = lax.axis_index("core").reshape(1).astype(jnp.int32)
    whole = pl.BlockSpec(memory_space=pltpu.VMEM)
    shape = jax.ShapeDtypeStruct((8, 2, share, 32 * k), jnp.bfloat16)
    others = [lax.ppermute(part, "core", shift(2, 1)) for part in held]
    found = []
    for own, other in zip(held, others):
        if found:
            other, found[-1] = lax.optimization_barrier((other, found[-1]))
        both = pl.pallas_call(
            lay_out,
            in_specs=[pl.BlockSpec(memory_space=pltpu.SMEM), whole, whole],
            out_specs=[whole, whole],
            out_shape=[shape, shape],
            compiler_params=pltpu.CompilerParams(vmem_limit_bytes=16 * 1024 * 1024),
            name="lay_out",
        )(core, own, other)
        found.append(tuple(half.reshape(16 * share, 32 * k) for half in both))
    return found, right


def on_device(points, frequencies, phases, feature_weights, observed, factor):
    blocks, share, width = observed.shape
    samples = width // 4
    size = 16 * share

    sides = []
    for block in range(blocks):
        features = feature_rows(points[:, block], frequencies, phases)
        prior = jnp.dot(features, feature_weights, preferred_element_type=jnp.float32)
        sides.append(observed[block] - prior)
    send = jnp.stack(sides).reshape(blocks, share, 4, samples).transpose(0, 2, 1, 3)
    send = send.reshape(16, share * samples // 128, 128)

    def send_sides(send):
        came = lax.all_to_all(send, ROW, 0, 0, tiled=True)
        return came.reshape(size, samples).T

    (diagonal, beside, third), right = gather_blocks(factor, send, send_sides)

    here = lax.axis_index("x")

    def move(value, source, target):
        return lax.ppermute(value, "x", [(source, target)])

    first = times(right, diagonal, 1)
    near = move(first, 0, 1)
    skip = move(first, 0, 2)
    far = move(times(first, third, 1), 0, 3)
    second = times(right - times(near, beside, 1), diagonal, 1)
    near = move(second, 1, 2)
    skip_on = move(second, 1, 3)
    base = right - times(skip, third, 1)
    solved = times(base - times(near, beside, 1), diagonal, 1)
    near = move(solved, 2, 3)
    base = right - far - times(skip_on, third, 1)
    last = times(base - times(near, beside, 1), diagonal, 1)
    mine = jnp.where(here == 0, first, jnp.where(here == 1, second, jnp.where(here == 2, solved, last)))

    fourth = times(mine, diagonal, 0)
    near = move(times(fourth, beside, 0), 3, 2)
    far = move(fourth, 3, 0)
    skip = move(times(fourth, third, 0), 3, 1)
    answer = times(mine - near, diagonal, 0)
    near = move(times(answer, beside, 0), 2, 1)
    skip_on = move(times(answer, third, 0), 2, 0)
    second = times(mine - skip - near, diagonal, 0)
    near = move(times(second, beside, 0), 1, 0)
    base = mine - skip_on - times(far, third, 0)
    first = times(base - near, diagonal, 0)
    result = jnp.where(here == 0, first, jnp.where(here == 1, second, jnp.where(here == 2, answer, fourth)))

    send = result.T.reshape(16, share * samples // 128, 128)
    came = lax.all_to_all(send, ROW, 0, 0, tiled=True)
    came = came.reshape(blocks, 4, share, samples).transpose(0, 2, 1, 3)
    return came.reshape(blocks, share, width)


def solution(mesh):
    fine = Mesh(mesh.devices.reshape(tuple(SPLIT.values())), tuple(SPLIT))
    in_specs = (
        P(None, None, ROW),
        P(),
        P(),
        P(None, COL),
        P(None, ROW, COL),
        P(None, ROW, COL),
    )
    return jax.shard_map(
        on_device, mesh=fine, in_specs=in_specs, out_specs=P(None, ROW, COL), check_vma=False
    )
```

```python
import math

import jax
import jax.numpy as jnp
import numpy as np
from jax import lax
from jax.experimental import pallas as pl
from jax.experimental.pallas import tpu as pltpu
from jax.sharding import Mesh
from jax.sharding import PartitionSpec as P

highest = lax.Precision.HIGHEST

SPLIT = {"x": 4, "zh": 2, "core": 2, "y": 8, "zl": 4}
ROW = ("x", "zh", "core")
COL = ("y", "zl")
Z = ("zh", "zl")

HELD = (
    ((0, 0), (3, 0), (2, 0)),
    ((1, 1), (1, 0), (3, 1)),
    ((2, 2), (2, 1), (2, 0)),
    ((3, 3), (3, 2), (3, 1)),
)
PARTS = ((0, 8), (8, 16), (16, 20))


def cos_coefficients():
    count = 8
    nodes = 0.125 * (1.0 - np.cos((np.arange(count) + 0.5) * np.pi / count))
    return np.polyfit(nodes * 8.0 - 1.0, np.cos(2.0 * np.pi * np.sqrt(nodes)), count - 1), nodes


def polynomial():
    fitted, _ = cos_coefficients()
    shifted = np.poly1d(fitted)(np.poly1d([8.0, -1.0]))
    return [float(c) for c in shifted.coeffs]


def feature_rows(points, frequencies, phases):
    turn = 1.0 / (2.0 * math.pi)
    rows = points.reshape(points.shape[0], -1)
    turns = lax.dot_general(
        rows, frequencies * turn, (((0,), (0,)), ((), ())), precision=highest, preferred_element_type=jnp.float32
    )
    turns = turns + phases * turn
    part = turns - jnp.round(turns)
    square = part * part
    scale = math.sqrt(2.0 / frequencies.shape[1])
    coefficients = polynomial()
    value = jnp.full_like(square, scale * coefficients[0])
    for c in coefficients[1:]:
        value = value * square + scale * c
    return value.astype(jnp.bfloat16)


def shift(size, step):
    return [(i, (i + step) % size) for i in range(size)]


def ring_gather(unit, axis, size, parts, beside):
    here = lax.axis_index(axis)
    held = [jnp.zeros((size, end - start) + unit.shape[1:], unit.dtype) for start, end in parts]

    def put(held, piece, step):
        at = (lax.rem(here + step + size, size),) + (0,) * unit.ndim
        return [
            lax.dynamic_update_slice(part, piece[None, start:end], at) for part, (start, end) in zip(held, parts)
        ]

    held = put(held, unit, 0)
    up = down = unit
    result = None
    for step in range(1, size // 2):
        up = lax.ppermute(up, axis, shift(size, 1))
        down = lax.ppermute(down, axis, shift(size, -1))
        if step == 1:
            result = beside()
            down, result = lax.optimization_barrier((down, result))
        held = put(held, up, -step)
        held = put(held, down, step)
    half = unit.shape[0] // 2
    first = lax.ppermute(up[:half], axis, shift(size, 1))
    second = lax.ppermute(down[half:], axis, shift(size, -1))
    return put(held, jnp.concatenate([first, second], 0), size // 2), result


def halves(value):
    high = lax.reduce_precision(value, 8, 7)
    return high.astype(jnp.bfloat16), (value - high).astype(jnp.bfloat16)


def times(left, right, contract):
    n = left.shape[0]
    high, low = halves(left)
    dims = (((1,), (contract,)), ((), ()))
    both = lax.dot_general(jnp.concatenate([high, low], 0), right[0], dims, preferred_element_type=jnp.float32)
    rest = lax.dot_general(high, right[1], dims, preferred_element_type=jnp.float32)
    return both[:n] + both[n:] + rest


def spread_lanes(came_ref, unit_ref):
    for place in range(8):
        pieces = [came_ref[4 * place + zl] for zl in range(4)]
        for slot in range(3):
            for rows, base, start in ((slice(0, 48), slot, 0), (slice(16 * slot, 16 * slot + 16), 3, 48)):
                found = None
                for zl in range(4):
                    part = pieces[zl][rows]
                    moved = (zl - base) * 32 % 128
                    part = pltpu.roll(part, moved, 1) if moved else part
                    group = lax.broadcasted_iota(jnp.int32, part.shape, 1) // 32
                    found = part if found is None else jnp.where(group == zl, part, found)
                unit_ref[8 * slot + place, start : start + found.shape[0], :] = found


def lay_out(core_ref, own_ref, other_ref, high_ref, low_ref):
    core = core_ref[0]

    def one(place, carry):
        for ref, at in ((own_ref, core), (other_ref, 1 - core)):
            for y in range(ref.shape[0]):
                value = ref[y, place]
                high = value.astype(jnp.bfloat16)
                high_ref[place, at, :, 128 * y : 128 * y + 128] = high
                low_ref[place, at, :, 128 * y : 128 * y + 128] = (value - high.astype(jnp.float32)).astype(jnp.bfloat16)
        return carry

    lax.fori_loop(0, own_ref.shape[1], one, 0)


def gather_blocks(factor, sides, send_sides):
    blocks, share, lanes = factor.shape
    k = lanes // blocks
    empty = jnp.zeros((share, k), factor.dtype)

    def piece(at):
        return empty if at is None else factor[at[0], :, at[1] * k : (at[1] + 1) * k]

    cut = share * 3 // 4
    send = []
    for slots in HELD:
        parts = [piece(at) for at in slots]
        rest = jnp.concatenate([part[cut:] for part in parts], 0)
        send.append(jnp.concatenate([part[:cut] for part in parts] + [rest], 1))
    send = jnp.broadcast_to(jnp.stack(send)[:, None], (4, 8, cut, 4 * k)).reshape(32, cut, 4 * k)
    came = lax.all_to_all(send, ("x",) + Z, 0, 0, tiled=True)
    unit = pl.pallas_call(
        spread_lanes,
        out_shape=jax.ShapeDtypeStruct((24, share, 4 * k), jnp.float32),
        compiler_params=pltpu.CompilerParams(vmem_limit_bytes=16 * 1024 * 1024),
        name="spread_lanes",
    )(came)
    upper = lax.axis_index("x") >= 2
    unit = jnp.concatenate([unit[:16], jnp.where(upper, unit[16:20], unit[20:])], 0)
    unit, sides = lax.optimization_barrier((unit, sides))
    held, right = ring_gather(unit, "y", 8, PARTS, lambda: send_sides(sides))
    core = lax.axis_index("core").reshape(1).astype(jnp.int32)
    whole = pl.BlockSpec(memory_space=pltpu.VMEM)
    others = [lax.ppermute(part, "core", shift(2, 1)) for part in held]
    found = []
    for own, other in zip(held, others):
        if found:
            other, found[-1] = lax.optimization_barrier((other, found[-1]))
        shape = jax.ShapeDtypeStruct((own.shape[1], 2, share, 32 * k), jnp.bfloat16)
        both = pl.pallas_call(
            lay_out,
            in_specs=[pl.BlockSpec(memory_space=pltpu.SMEM), whole, whole],
            out_specs=[whole, whole],
            out_shape=[shape, shape],
            compiler_params=pltpu.CompilerParams(vmem_limit_bytes=16 * 1024 * 1024),
            name="lay_out",
        )(core, own, other)
        found.append(tuple(half.reshape(-1, 32 * k) for half in both))
    return found, right


def on_device(points, frequencies, phases, feature_weights, observed, factor):
    blocks, share, width = observed.shape
    samples = width // 4
    size = 16 * share

    sides = []
    for block in range(blocks):
        features = feature_rows(points[:, block], frequencies, phases)
        prior = jnp.dot(features, feature_weights, preferred_element_type=jnp.float32)
        sides.append(observed[block] - prior)
    send = jnp.stack(sides).reshape(blocks, share, 4, samples).transpose(0, 2, 1, 3)
    send = send.reshape(16, share * samples // 128, 128)

    def send_sides(send):
        came = lax.all_to_all(send, ROW, 0, 0, tiled=True)
        return came.reshape(size, samples).T

    (diagonal, beside, third), right = gather_blocks(factor, send, send_sides)

    here = lax.axis_index("x")

    def move(value, source, target):
        return lax.ppermute(value, "x", [(source, target)])

    def beyond(value):
        return jnp.concatenate([value, times(value, third, 1)], 1)

    def whole_third(skip):
        return jnp.concatenate([times(skip[:, :size], third, 1), skip[:, size:]], 1)

    def beyond_back(value):
        return jnp.concatenate([times(value[:, : size // 2], third, 0), value[:, size // 2 :]], 1)

    def whole_third_back(skip):
        return skip[:, :size] + times(skip[:, size:], third, 0)

    first = times(right, diagonal, 1)
    near = move(first, 0, 1)
    skip = move(beyond(first), 0, 2)
    far = move(times(first, beside, 1), 0, 3)
    second = times(right - times(near, beside, 1), diagonal, 1)
    near = move(second, 1, 2)
    skip_on = move(beyond(second), 1, 3)
    base = right - whole_third(skip)
    solved = times(base - times(near, beside, 1), diagonal, 1)
    near = move(solved, 2, 3)
    base = right - far - whole_third(skip_on)
    last = times(base - times(near, beside, 1), diagonal, 1)
    mine = jnp.where(here == 0, first, jnp.where(here == 1, second, jnp.where(here == 2, solved, last)))

    fourth = times(mine, diagonal, 0)
    near = move(times(fourth, beside, 0), 3, 2)
    far = move(fourth, 3, 0)
    skip = move(beyond_back(fourth), 3, 1)
    answer = times(mine - near, diagonal, 0)
    near = move(times(answer, beside, 0), 2, 1)
    skip_on = move(beyond_back(answer), 2, 0)
    second = times(mine - whole_third_back(skip) - near, diagonal, 0)
    near = move(times(second, beside, 0), 1, 0)
    base = mine - whole_third_back(skip_on) - times(far, beside, 0)
    first = times(base - near, diagonal, 0)
    result = jnp.where(here == 0, first, jnp.where(here == 1, second, jnp.where(here == 2, answer, fourth)))

    send = result.T.reshape(16, share * samples // 128, 128)
    came = lax.all_to_all(send, ROW, 0, 0, tiled=True)
    came = came.reshape(blocks, 4, share, samples).transpose(0, 2, 1, 3)
    return came.reshape(blocks, share, width)


def solution(mesh):
    fine = Mesh(mesh.devices.reshape(tuple(SPLIT.values())), tuple(SPLIT))
    in_specs = (
        P(None, None, ROW),
        P(),
        P(),
        P(None, COL),
        P(None, ROW, COL),
        P(None, ROW, COL),
    )
    return jax.shard_map(
        on_device, mesh=fine, in_specs=in_specs, out_specs=P(None, ROW, COL), check_vma=False
    )
```

```python
import math

import jax
import jax.numpy as jnp
import numpy as np
from jax import lax
from jax.experimental import pallas as pl
from jax.experimental.pallas import tpu as pltpu
from jax.sharding import Mesh
from jax.sharding import PartitionSpec as P

highest = lax.Precision.HIGHEST

SPLIT = {"x": 4, "zh": 2, "core": 2, "y": 8, "zl": 4}
ROW = ("x", "zh", "core")
COL = ("y", "zl")
Z = ("zh", "zl")

HELD = (
    ((0, 0), (3, 0), (2, 0)),
    ((1, 1), (1, 0), (3, 1)),
    ((2, 2), (2, 1), (2, 0)),
    ((3, 3), (3, 2), (3, 1)),
)
PARTS = ((0, 8), (8, 16), (16, 20))


def cos_coefficients():
    count = 8
    nodes = 0.125 * (1.0 - np.cos((np.arange(count) + 0.5) * np.pi / count))
    return np.polyfit(nodes * 8.0 - 1.0, np.cos(2.0 * np.pi * np.sqrt(nodes)), count - 1), nodes


def polynomial():
    fitted, _ = cos_coefficients()
    shifted = np.poly1d(fitted)(np.poly1d([8.0, -1.0]))
    return [float(c) for c in shifted.coeffs]


def feature_rows(points, frequencies, phases):
    turn = 1.0 / (2.0 * math.pi)
    rows = points.reshape(points.shape[0], -1)
    turns = lax.dot_general(
        rows, frequencies * turn, (((0,), (0,)), ((), ())), precision=highest, preferred_element_type=jnp.float32
    )
    turns = turns + phases * turn
    part = turns - jnp.round(turns)
    square = part * part
    scale = math.sqrt(2.0 / frequencies.shape[1])
    coefficients = polynomial()
    value = jnp.full_like(square, scale * coefficients[0])
    for c in coefficients[1:]:
        value = value * square + scale * c
    return value.astype(jnp.bfloat16)


def shift(size, step):
    return [(i, (i + step) % size) for i in range(size)]


def ring_gather(unit, axis, size, parts, beside):
    here = lax.axis_index(axis)
    held = [jnp.zeros((size, end - start) + unit.shape[1:], unit.dtype) for start, end in parts]

    def put(held, piece, step):
        at = (lax.rem(here + step + size, size),) + (0,) * unit.ndim
        return [
            lax.dynamic_update_slice(part, piece[None, start:end], at) for part, (start, end) in zip(held, parts)
        ]

    held = put(held, unit, 0)
    up = down = unit
    result = None
    for step in range(1, size // 2):
        up = lax.ppermute(up, axis, shift(size, 1))
        down = lax.ppermute(down, axis, shift(size, -1))
        if step == 1:
            result = beside()
            down, result = lax.optimization_barrier((down, result))
        held = put(held, up, -step)
        held = put(held, down, step)
    half = unit.shape[0] // 2
    first = lax.ppermute(up[:half], axis, shift(size, 1))
    second = lax.ppermute(down[half:], axis, shift(size, -1))
    return put(held, jnp.concatenate([first, second], 0), size // 2), result


def halves(value):
    high = lax.reduce_precision(value, 8, 7)
    return high.astype(jnp.bfloat16), (value - high).astype(jnp.bfloat16)


def times(left, right, contract):
    n = left.shape[0]
    high, low = halves(left)
    dims = (((1,), (contract,)), ((), ()))
    both = lax.dot_general(jnp.concatenate([high, low], 0), right[0], dims, preferred_element_type=jnp.float32)
    rest = lax.dot_general(high, right[1], dims, preferred_element_type=jnp.float32)
    return both[:n] + both[n:] + rest


def spread_lanes(came_ref, unit_ref):
    for place in range(8):
        pieces = [came_ref[4 * place + zl] for zl in range(4)]
        for slot in range(3):
            for rows, base, start in ((slice(0, 48), slot, 0), (slice(16 * slot, 16 * slot + 16), 3, 48)):
                found = None
                for zl in range(4):
                    part = pieces[zl][rows]
                    moved = (zl - base) * 32 % 128
                    part = pltpu.roll(part, moved, 1) if moved else part
                    group = lax.broadcasted_iota(jnp.int32, part.shape, 1) // 32
                    found = part if found is None else jnp.where(group == zl, part, found)
                unit_ref[8 * slot + place, start : start + found.shape[0], :] = found


def lay_out(core_ref, own_ref, other_ref, high_ref, low_ref):
    core = core_ref[0]

    def one(place, carry):
        for ref, at in ((own_ref, core), (other_ref, 1 - core)):
            for y in range(ref.shape[0]):
                value = ref[y, place]
                high = value.astype(jnp.bfloat16)
                high_ref[place, at, :, 128 * y : 128 * y + 128] = high
                low_ref[place, at, :, 128 * y : 128 * y + 128] = (value - high.astype(jnp.float32)).astype(jnp.bfloat16)
        return carry

    lax.fori_loop(0, own_ref.shape[1], one, 0)


def gather_blocks(factor, sides, send_sides):
    blocks, share, lanes = factor.shape
    k = lanes // blocks
    empty = jnp.zeros((share, k), factor.dtype)

    def piece(at):
        return empty if at is None else factor[at[0], :, at[1] * k : (at[1] + 1) * k]

    cut = share * 3 // 4
    send = []
    for slots in HELD:
        parts = [piece(at) for at in slots]
        rest = jnp.concatenate([part[cut:] for part in parts], 0)
        send.append(jnp.concatenate([part[:cut] for part in parts] + [rest], 1))
    send = jnp.broadcast_to(jnp.stack(send)[:, None], (4, 8, cut, 4 * k)).reshape(32, cut, 4 * k)
    came = lax.all_to_all(send, ("x",) + Z, 0, 0, tiled=True)
    unit = pl.pallas_call(
        spread_lanes,
        out_shape=jax.ShapeDtypeStruct((24, share, 4 * k), jnp.float32),
        compiler_params=pltpu.CompilerParams(vmem_limit_bytes=16 * 1024 * 1024),
        name="spread_lanes",
    )(came)
    upper = lax.axis_index("x") >= 2
    unit = jnp.concatenate([unit[:16], jnp.where(upper, unit[16:20], unit[20:])], 0)
    unit, sides = lax.optimization_barrier((unit, sides))
    held, right = ring_gather(unit, "y", 8, PARTS, lambda: send_sides(sides))
    core = lax.axis_index("core").reshape(1).astype(jnp.int32)
    whole = pl.BlockSpec(memory_space=pltpu.VMEM)
    others = [lax.ppermute(part, "core", shift(2, 1)) for part in held]

    def lay(slot, after):
        own, other = held[slot], others[slot]
        if after is not None:
            other, after = lax.optimization_barrier((other, after))
        shape = jax.ShapeDtypeStruct((own.shape[1], 2, share, 32 * k), jnp.bfloat16)
        both = pl.pallas_call(
            lay_out,
            in_specs=[pl.BlockSpec(memory_space=pltpu.SMEM), whole, whole],
            out_specs=[whole, whole],
            out_shape=[shape, shape],
            compiler_params=pltpu.CompilerParams(vmem_limit_bytes=16 * 1024 * 1024),
            name="lay_out",
        )(core, own, other)
        return tuple(half.reshape(-1, 32 * k) for half in both)

    return lay, right


def on_device(points, frequencies, phases, feature_weights, observed, factor):
    blocks, share, width = observed.shape
    samples = width // 4
    size = 16 * share

    sides = []
    for block in range(blocks):
        features = feature_rows(points[:, block], frequencies, phases)
        prior = jnp.dot(features, feature_weights, preferred_element_type=jnp.float32)
        sides.append(observed[block] - prior)
    send = jnp.stack(sides).reshape(blocks, share, 4, samples).transpose(0, 2, 1, 3)
    send = send.reshape(16, share * samples // 128, 128)

    def send_sides(send):
        came = lax.all_to_all(send, ROW, 0, 0, tiled=True)
        return came.reshape(size, samples).T

    lay, right = gather_blocks(factor, send, send_sides)
    diagonal = lay(0, None)

    here = lax.axis_index("x")

    def move(value, source, target):
        return lax.ppermute(value, "x", [(source, target)])

    def beyond(value):
        return jnp.concatenate([value, times(value, third, 1)], 1)

    def whole_third(skip):
        return jnp.concatenate([times(skip[:, :size], third, 1), skip[:, size:]], 1)

    def beyond_back(value):
        return jnp.concatenate([times(value[:, : size // 2], third, 0), value[:, size // 2 :]], 1)

    def whole_third_back(skip):
        return skip[:, :size] + times(skip[:, size:], third, 0)

    first = times(right, diagonal, 1)
    near = move(first, 0, 1)
    beside = lay(1, first)
    third = lay(2, beside)
    skip = move(beyond(first), 0, 2)
    second = times(right - times(near, beside, 1), diagonal, 1)
    near = move(second, 1, 2)
    late, _ = lax.optimization_barrier((first, second))
    far = move(times(late, beside, 1), 0, 3)
    skip_on = move(beyond(second), 1, 3)
    base = right - whole_third(skip)
    solved = times(base - times(near, beside, 1), diagonal, 1)
    near = move(solved, 2, 3)
    base = right - far - whole_third(skip_on)
    last = times(base - times(near, beside, 1), diagonal, 1)
    mine = jnp.where(here == 0, first, jnp.where(here == 1, second, jnp.where(here == 2, solved, last)))

    fourth = times(mine, diagonal, 0)
    near = move(times(fourth, beside, 0), 3, 2)
    far = move(fourth, 3, 0)
    skip = move(beyond_back(fourth), 3, 1)
    answer = times(mine - near, diagonal, 0)
    near = move(times(answer, beside, 0), 2, 1)
    skip_on = move(beyond_back(answer), 2, 0)
    second = times(mine - whole_third_back(skip) - near, diagonal, 0)
    near = move(times(second, beside, 0), 1, 0)
    base = mine - whole_third_back(skip_on) - times(far, beside, 0)
    first = times(base - near, diagonal, 0)
    result = jnp.where(here == 0, first, jnp.where(here == 1, second, jnp.where(here == 2, answer, fourth)))

    send = result.T.reshape(16, share * samples // 128, 128)
    came = lax.all_to_all(send, ROW, 0, 0, tiled=True)
    came = came.reshape(blocks, 4, share, samples).transpose(0, 2, 1, 3)
    return came.reshape(blocks, share, width)


def solution(mesh):
    fine = Mesh(mesh.devices.reshape(tuple(SPLIT.values())), tuple(SPLIT))
    in_specs = (
        P(None, None, ROW),
        P(),
        P(),
        P(None, COL),
        P(None, ROW, COL),
        P(None, ROW, COL),
    )
    return jax.shard_map(
        on_device, mesh=fine, in_specs=in_specs, out_specs=P(None, ROW, COL), check_vma=False
    )
```
